256 devices in a mesh: dp: 16 (over z_lo, x, core), expert: 16 (over y, z_hi).
Axes of the slice: x: 4, y: 4, z: 8 (z_hi: 4, z_lo: 2; z = z_hi * 2 + z_lo), core: 2. Of those that a mesh axis runs over, the one named last changes fastest.
Arguments:
- tokens: bfloat16 [32768, 2048], P(('dp', 'expert')), may hold values from -6 to 6
- expert_ids: int32 [32768, 4], P(('dp', 'expert')), may hold values from 0 to 15, all different within a row
- gate_fixed: int32 [32768, 4], P(('dp', 'expert')), may hold values from 1 to 65535
- hot_ids: int32 [1], replicated, may hold values from 0 to 15
- w_gate: bfloat16 [16, 2048, 768], P('expert', 'dp'), may hold values from -0.125 to 0.125
- w_up: bfloat16 [16, 2048, 768], P('expert', 'dp'), may hold values from -0.125 to 0.125
- w_down: bfloat16 [16, 768, 2048], P('expert', None, 'dp'), may hold values from -0.21875 to 0.21875
Outputs:
- mixed: bfloat16 [32768, 2048], P(('dp', 'expert'))
The draws below stay inside these ranges and needn't reach their ends.
Inputs may be any that keep to these rules, and one draw needn't show every extreme that they name: `expert_ids`: each token names 4 different experts, and every expert is named by some token. `gate_fixed`: an entry g stands for the gate weight g / 65536. `hot_ids`: the same shadowed expert holds for all data groups.
All inputs are finite; a program needn't handle non-finite values.
Results may differ from the reference program's by a relative error of at most 0.0065.
Values may be sent and summed in bfloat16 or wider, within the bound.
No kernel may reach another device: no remote copies, remote signals or barrier semaphores. Data moves between devices by JAX's collectives and lax.ppermute only.
A program may use at most 128 MiB of HBM per device.

```python
import jax
import jax.numpy as jnp
from jax import lax

D = 2048
FF = 768
TOP = 4
TOK_DEV = 128
EXPERTS = 16
CAP = 32
TOKENS = 32768


def set_ends(values, key, least, top_value):
    longest = values.shape.index(max(values.shape))
    spots = []
    for shift in (0, 1):
        where = [jax.random.randint(jax.random.fold_in(key, axis), (), 0, length) for axis, length in enumerate(values.shape)]
        where[longest] = (where[longest] + shift) % values.shape[longest]
        spots.append(tuple(where))
    return values.at[spots[0]].set(least).at[spots[1]].set(top_value)


def level_of(rng, shape, shards, smallest, high):
    gain = 1.0
    for position, shards_of in shards:
        heights = jax.random.uniform(jax.random.fold_in(jax.random.fold_in(rng, 6), position), (shards_of,), jnp.float32, smallest / len(shards), high / len(shards))
        gain = gain * jnp.repeat(jnp.exp(heights), shape[position] // shards_of).reshape((-1,) + (1,) * (len(shape) - 1 - position))
    return gain


def choose_distinct(own_key, rows, count, top, lift):
    order = jax.random.permutation(jax.random.fold_in(own_key, 1), count)
    boost = order
    for power in range(3):
        boost = boost * boost // count
    boost = boost * lift // count
    tickets = jax.random.randint(jax.random.fold_in(own_key, 2), (rows, count), 0, 4096) + boost
    fixed_rows = jax.random.permutation(jax.random.fold_in(own_key, 3), rows)[jnp.arange(count) % rows]
    tickets = jnp.where(jnp.arange(rows)[:, None] == fixed_rows[None, :], 1 << 14, tickets)
    priority = tickets * count + jnp.arange(count)
    return lax.top_k(priority.astype(jnp.int32), top)[1].astype(jnp.int32)


def noise(key, shape, scale, reach, pieces=(), kind=jnp.bfloat16):
    level = level_of(key, shape, pieces, -0.22, 0.18) if pieces else 1.0
    values = jax.random.normal(key, shape, jnp.float32) * scale * level
    return jnp.minimum(jnp.maximum(values, -reach), reach).astype(kind)


def setup_inputs(seed: int = 0) -> dict:
    seeds = jax.random.split(jax.random.key(seed), 8)
    tokens = noise(seeds[0], (TOKENS, D), 1.0, 6.0, ((0, 256),))
    expert_ids = choose_distinct(seeds[1], TOKENS, EXPERTS, TOP, 4096)
    gate_fixed = set_ends(jax.random.randint(seeds[2], (TOKENS, TOP), 1, 65536), jax.random.fold_in(seeds[2], 1), 1, 65535).astype(jnp.int32)
    hot_ids = jax.random.randint(seeds[3], (1,), 0, EXPERTS).astype(jnp.int32)
    w_gate = noise(seeds[4], (EXPERTS, D, FF), D ** -0.5, 0.125, ((0, 16), (1, 16)))
    w_up = noise(seeds[5], (EXPERTS, D, FF), D ** -0.5, 0.125, ((0, 16), (1, 16)))
    w_down = noise(seeds[6], (EXPERTS, FF, D), FF ** -0.5, 0.21875, ((0, 16), (2, 16)))
    return {"tokens": tokens, "expert_ids": expert_ids, "gate_fixed": gate_fixed, "hot_ids": hot_ids, "w_gate": w_gate, "w_up": w_up, "w_down": w_down}


def expert_mlp(rows, gate_mat, up_mat, down_mat):
    gated = jnp.dot(rows, gate_mat, preferred_element_type=jnp.float32)
    upward = jnp.dot(rows, up_mat, preferred_element_type=jnp.float32)
    hidden = (jax.nn.silu(gated) * upward).astype(jnp.bfloat16)
    return jnp.dot(hidden, down_mat, preferred_element_type=jnp.float32).astype(jnp.bfloat16)


def reference(tokens, expert_ids, gate_fixed, hot_ids, w_gate, w_up, w_down):
    count = tokens.shape[0]
    width = tokens.shape[1]
    blocks = count // TOK_DEV
    per_block = TOK_DEV * TOP
    hot_id = hot_ids[0]
    routed = expert_ids.reshape(blocks, per_block)
    columns = jnp.arange(EXPERTS).astype(jnp.int32)
    onehot = (routed[:, :, None] == columns[None, None, :]).astype(jnp.int32)
    ranking = jnp.sum((jnp.cumsum(onehot, axis=1) - 1) * onehot, axis=2)
    is_hot = routed == hot_id
    is_sent = jnp.logical_and(jnp.logical_not(is_hot), ranking < CAP)
    scaled = gate_fixed.reshape(blocks, per_block).astype(jnp.float32) / 65536.0
    block_ids = jnp.arange(blocks).astype(jnp.int32)[:, None]
    owners = block_ids * TOK_DEV + (jnp.arange(per_block).astype(jnp.int32) // TOP)[None, :]
    rows_index = jnp.broadcast_to(block_ids, (blocks, per_block))
    padded = jnp.concatenate([tokens, jnp.zeros((1, width), tokens.dtype)], 0)

    def add_expert(expert, totals):
        mine = jnp.logical_and(is_sent, routed == expert)
        place = jnp.where(mine, ranking, CAP)
        table = jnp.full((blocks, CAP + 1), count, jnp.int32).at[rows_index, place].set(owners)
        table = table[:, :CAP].reshape(-1)
        factor = jnp.zeros((blocks, CAP + 1), jnp.float32).at[rows_index, place].set(scaled)
        factor = factor[:, :CAP].reshape(-1)
        result = expert_mlp(padded[table], w_gate[expert], w_up[expert], w_down[expert])
        return totals.at[table].add(factor[:, None] * result.astype(jnp.float32), mode="drop")

    totals = lax.fori_loop(0, EXPERTS, add_expert, jnp.zeros((count, width), jnp.float32))
    hot_scale = jnp.sum(jnp.where(is_hot, scaled, 0.0).reshape(count, TOP), axis=1)
    hot_gate = w_gate[hot_id]
    hot_up = w_up[hot_id]
    hot_down = w_down[hot_id]

    def hot_block(part):
        return expert_mlp(part, hot_gate, hot_up, hot_down)

    hot_rows = lax.map(hot_block, tokens.reshape(blocks, TOK_DEV, width)).reshape(count, width)
    mixed = totals + hot_scale[:, None] * hot_rows.astype(jnp.float32)
    return mixed.astype(jnp.bfloat16)
```

```python
import jax
import jax.numpy as jnp
from jax import lax
from jax.experimental import pallas as pl
from jax.experimental.pallas import tpu as pltpu
from jax.sharding import Mesh, PartitionSpec as P

AXES = ("zlo", "x", "core", "y", "zhi")
SIZES = (2, 4, 2, 4, 4)
TOK, WIDTH, FF, EXPERTS, CAP = 128, 2048, 768, 16, 32
SLOTS = EXPERTS * CAP
ROWS = 384
BF, F32, I32 = jnp.bfloat16, jnp.float32, jnp.int32


def dot(a, b):
    return jnp.dot(a, b, preferred_element_type=F32)


def vmem(count):
    return [pl.BlockSpec(memory_space=pltpu.VMEM)] * count


SMEM = pl.BlockSpec(memory_space=pltpu.SMEM)
PARAMS = pltpu.CompilerParams(vmem_limit_bytes=44 * 2**20)


def expand():
    expert = lax.broadcasted_iota(I32, (EXPERTS, SLOTS), 0)
    slot = lax.broadcasted_iota(I32, (EXPERTS, SLOTS), 1)
    return (lax.shift_right_logical(slot, 5) == expert).astype(F32).astype(BF)


def slot_mask(ids, hot):
    column = lax.broadcasted_iota(I32, (TOK, EXPERTS), 1)
    member = ids[:, 0:1] == column
    for k in range(1, 4):
        member = jnp.logical_or(member, ids[:, k : k + 1] == column)
    row = lax.broadcasted_iota(I32, (TOK, TOK), 0)
    col = lax.broadcasted_iota(I32, (TOK, TOK), 1)
    earlier = (col < row).astype(F32).astype(BF)
    rank = dot(earlier, member.astype(F32).astype(BF))
    rank = jnp.where(jnp.logical_and(member, column != hot), rank, -1.0)
    wide = dot(rank.astype(BF), expand())
    place = jnp.bitwise_and(lax.broadcasted_iota(I32, (TOK, SLOTS), 1), CAP - 1)
    return wide == place.astype(F32)


def dispatch_kernel(hot_ref, ids_ref, tok_ref, out_ref):
    mask = slot_mask(ids_ref[...], hot_ref[0]).astype(F32).astype(BF)
    out_ref[...] = lax.dot_general(
        mask, tok_ref[...], (((0,), (0,)), ((), ())), preferred_element_type=F32
    ).astype(BF)


def combine_kernel(hot_ref, ids_ref, gate_ref, back_ref, hot_rows_ref, out_ref):
    ids, gates, hot = ids_ref[...], gate_ref[...], hot_ref[0]
    mask = slot_mask(ids, hot)
    column = lax.broadcasted_iota(I32, (TOK, EXPERTS), 1)
    per_expert = jnp.zeros((TOK, EXPERTS), I32)
    hot_gate = jnp.zeros((TOK, 1), I32)
    for k in range(4):
        ids_k, gates_k = ids[:, k : k + 1], gates[:, k : k + 1]
        per_expert = per_expert + jnp.where(ids_k == column, gates_k, 0)
        hot_gate = hot_gate + jnp.where(ids_k == hot, gates_k, 0)
    high = lax.shift_right_logical(per_expert, 8).astype(F32).astype(BF)
    low = jnp.bitwise_and(per_expert, 255).astype(F32).astype(BF)
    spread = expand()
    high = jnp.where(mask, dot(high, spread), 0.0).astype(BF)
    low = jnp.where(mask, dot(low, spread), 0.0).astype(BF)
    back = back_ref[...]
    mixed = dot(high, back) * (1.0 / 256.0) + dot(low, back) * (1.0 / 65536.0)
    hot_scale = hot_gate.astype(F32) * (1.0 / 65536.0)
    out_ref[...] = (mixed + hot_scale * hot_rows_ref[...].astype(F32)).astype(BF)


def silu_mul(gated, upward):
    return (gated / (1.0 + jnp.exp(-gated)) * upward).astype(BF)


def down_block(value):
    return jnp.concatenate([value[:, j * 128 : (j + 1) * 128] for j in range(6)], 0)


def own_kernel(place_ref, rows_ref, *refs):
    near, (first, second, first_o, second_o), out_ref, ordered, hidden = (
        refs[:14], refs[14:18], refs[18], refs[19], refs[20],
    )

    def gate(i, cols):
        if i < 14:
            return near[i][0:128, cols]
        return (first, first_o)[i - 14][0:128, cols]

    def up(i, cols):
        if i < 14:
            return near[i][128:256, cols]
        a, b = ((first, second), (first_o, second_o))[i - 14]
        return jnp.concatenate([a[128:192, cols], b[0:64, cols]], 0)

    def down(i):
        if i < 14:
            return down_block(near[i][256:384, :])
        return down_block((second, second_o)[i - 14][64:192, :])

    starts = [pl.multiple_of(place_ref[i] * 128, 128) for i in range(16)]
    for i in range(16):
        ordered[:, i * 128 : (i + 1) * 128] = rows_ref[:, pl.ds(starts[i], 128)]
    for n in range(3):
        cols = slice(n * 256, (n + 1) * 256)
        gated = dot(ordered[...], jnp.concatenate([gate(i, cols) for i in range(16)], 0))
        upward = dot(ordered[...], jnp.concatenate([up(i, cols) for i in range(16)], 0))
        hidden[:, cols] = silu_mul(gated, upward)
    for i in range(0, 16, 2):
        pair = dot(hidden[...], jnp.concatenate([down(i), down(i + 1)], 1)).astype(BF)
        out_ref[:, pl.ds(starts[i], 128)] = pair[:, 0:128]
        out_ref[:, pl.ds(starts[i + 1], 128)] = pair[:, 128:256]


def hot_kernel(tok_ref, w_ref, out_ref, hidden):
    def part(d, first, cols):
        zlo, x, core = d // 8, d // 2 % 4, d % 2
        return [w_ref[x, core, y, zlo, first : first + 32, cols] for y in range(4)]

    for n in range(3):
        cols = slice(n * 256, (n + 1) * 256)
        gated = dot(tok_ref[...], jnp.concatenate(sum([part(d, 0, cols) for d in range(16)], []), 0))
        upward = dot(tok_ref[...], jnp.concatenate(sum([part(d, 32, cols) for d in range(16)], []), 0))
        hidden[:, cols] = silu_mul(gated, upward)
    whole = slice(0, FF)
    for d in range(0, 16, 2):
        pair = [down_block(jnp.concatenate(part(d + c, 64, whole), 0)) for c in range(2)]
        out_ref[:, d * 128 : (d + 2) * 128] = dot(hidden[...], jnp.concatenate(pair, 1)).astype(BF)


def z_index(z):
    return (z % 2) * 4 + (z % 8) // 2


def z_shift(value, step):
    pairs = [(z_index(z), z_index(z + step)) for z in range(8)]
    return lax.ppermute(value, ("zlo", "zhi"), pairs)


def turn(value, axis, step):
    size = SIZES[AXES.index(axis)]
    return lax.ppermute(value, axis, [(i, (i + step) % size) for i in range(size)])


def other_core(value):
    return turn(value, "core", 1)


def gather_ring(own):
    up, down, found = own, own, [own]
    for _ in range(3):
        up, down = z_shift(up, 1), z_shift(down, -1)
        found += [up, down]
    half = ROWS // 2
    found += [z_shift(up[:half], 1), z_shift(down[half:], -1)]
    both = []
    for piece in found[:7]:
        both += [piece, other_core(piece)]
    return both + found[7:] + [other_core(piece) for piece in found[7:]]


def places():
    z = lax.axis_index("zhi") * 2 + lax.axis_index("zlo")
    core = lax.axis_index("core")
    out = []
    for step in (0, -1, 1, -2, 2, -3, 3, 4):
        from_z = lax.rem(z + step + 8, 8)
        index = lax.rem(from_z, 2) * 8 + from_z // 2 * 2
        out += [index + core, index + 1 - core]
    return jnp.stack(out).astype(I32)


def gather_hot(weights, hot):
    quarters = weights.reshape(3, 4, 32, FF).transpose(1, 0, 2, 3).reshape(ROWS, FF)
    mixed = lax.all_to_all(quarters, "y", split_axis=0, concat_axis=0, tiled=True)
    mine = lax.dynamic_slice_in_dim(mixed, hot // 4 * 96, 96, 0)
    before, after = turn(mine, "zhi", 1), turn(mine, "zhi", -1)
    across = turn(before, "zhi", 1)
    gap = lax.rem(hot % 4 - lax.axis_index("zhi") + 4, 4)
    mine = lax.select_n(gap, mine, after, across, before)
    theirs = turn(mine, "zlo", 1)
    zlo = lax.axis_index("zlo")
    both = jnp.stack([jnp.where(zlo == 0, mine, theirs), jnp.where(zlo == 0, theirs, mine)])
    whole = lax.all_gather(both, ("x", "core", "y"), axis=0, tiled=False)
    return whole.reshape(4, 2, 4, 2, 96, FF)


def on_device(tokens, expert_ids, gate_fixed, hot_ids, w_gate, w_up, w_down):
    hot = hot_ids[0]
    down = w_down[0].reshape(6, 128, 128).transpose(1, 0, 2).reshape(128, FF)
    weights = jnp.concatenate([w_gate[0], w_up[0], down], 0)
    swapped = lax.ppermute(
        weights, ("x", "zhi"), [(a * 4 + b, b * 4 + a) for a in range(4) for b in range(4)]
    )
    pieces = gather_ring(swapped)
    outgoing = pl.pallas_call(
        dispatch_kernel,
        out_shape=jax.ShapeDtypeStruct((SLOTS, WIDTH), BF),
        in_specs=[SMEM] + vmem(2),
        out_specs=vmem(1)[0],
        compiler_params=PARAMS,
    )(hot_ids, expert_ids, tokens)
    arrived = lax.all_to_all(outgoing, ("y", "x"), split_axis=0, concat_axis=0, tiled=True)
    hot_weights = gather_hot(weights, hot)
    result = pl.pallas_call(
        own_kernel,
        out_shape=jax.ShapeDtypeStruct((SLOTS, WIDTH), BF),
        in_specs=[SMEM] + vmem(1 + len(pieces)),
        out_specs=vmem(1)[0],
        scratch_shapes=[pltpu.VMEM((SLOTS, WIDTH), BF), pltpu.VMEM((SLOTS, FF), BF)],
        compiler_params=PARAMS,
        cost_estimate=pl.CostEstimate(flops=4_900_000_000, bytes_accessed=13_000_000, transcendentals=400_000),
    )(places(), arrived, *pieces)
    returned = lax.all_to_all(result, ("y", "x"), split_axis=0, concat_axis=0, tiled=True)
    hot_rows = pl.pallas_call(
        hot_kernel,
        out_shape=jax.ShapeDtypeStruct((TOK, WIDTH), BF),
        in_specs=vmem(2),
        out_specs=vmem(1)[0],
        scratch_shapes=[pltpu.VMEM((TOK, FF), BF)],
        compiler_params=PARAMS,
        cost_estimate=pl.CostEstimate(flops=1_300_000_000, bytes_accessed=10_000_000, transcendentals=100_000),
    )(tokens, hot_weights)
    return pl.pallas_call(
        combine_kernel,
        out_shape=jax.ShapeDtypeStruct((TOK, WIDTH), BF),
        in_specs=[SMEM] + vmem(4),
        out_specs=vmem(1)[0],
        compiler_params=PARAMS,
    )(hot_ids, expert_ids, gate_fixed, returned, hot_rows)


def solution(mesh):
    fine = Mesh(mesh.devices.reshape(SIZES), AXES)
    rows = P(("zlo", "x", "core", "y", "zhi"), None)
    slices = ("zlo", "x", "core")
    return jax.shard_map(
        on_device,
        mesh=fine,
        in_specs=(
            rows,
            rows,
            rows,
            P(),
            P(("y", "zhi"), slices, None),
            P(("y", "zhi"), slices, None),
            P(("y", "zhi"), None, slices),
        ),
        out_specs=rows,
        check_vma=False,
    )
```

```python
import jax
import jax.numpy as jnp
from jax import lax
from jax.experimental import pallas as pl
from jax.experimental.pallas import tpu as pltpu
from jax.sharding import Mesh, PartitionSpec as P

AXES = ("zlo", "x", "core", "y", "zhi")
SIZES = (2, 4, 2, 4, 4)
TOK, WIDTH, FF, EXPERTS, CAP = 128, 2048, 768, 16, 32
SLOTS = EXPERTS * CAP
BF, F32, I32 = jnp.bfloat16, jnp.float32, jnp.int32


def dot(a, b):
    return jnp.dot(a, b, preferred_element_type=F32)


def vmem(count):
    return [pl.BlockSpec(memory_space=pltpu.VMEM)] * count


def anywhere(count):
    return [pl.BlockSpec(memory_space=pltpu.HBM)] * count


SMEM = pl.BlockSpec(memory_space=pltpu.SMEM)
PARAMS = pltpu.CompilerParams(vmem_limit_bytes=24 * 2**20)


def expand():
    expert = lax.broadcasted_iota(I32, (EXPERTS, SLOTS), 0)
    slot = lax.broadcasted_iota(I32, (EXPERTS, SLOTS), 1)
    return (lax.shift_right_logical(slot, 5) == expert).astype(F32).astype(BF)


def slot_mask(ids, hot):
    column = lax.broadcasted_iota(I32, (TOK, EXPERTS), 1)
    member = ids[:, 0:1] == column
    for k in range(1, 4):
        member = jnp.logical_or(member, ids[:, k : k + 1] == column)
    row = lax.broadcasted_iota(I32, (TOK, TOK), 0)
    col = lax.broadcasted_iota(I32, (TOK, TOK), 1)
    earlier = (col < row).astype(F32).astype(BF)
    rank = dot(earlier, member.astype(F32).astype(BF))
    rank = jnp.where(jnp.logical_and(member, column != hot), rank, -1.0)
    wide = dot(rank.astype(BF), expand())
    place = jnp.bitwise_and(lax.broadcasted_iota(I32, (TOK, SLOTS), 1), CAP - 1)
    return wide == place.astype(F32)


def dispatch_kernel(hot_ref, ids_ref, tok_ref, out_ref):
    mask = slot_mask(ids_ref[...], hot_ref[0]).astype(F32).astype(BF)
    out_ref[...] = lax.dot_general(
        mask, tok_ref[...], (((0,), (0,)), ((), ())), preferred_element_type=F32
    ).astype(BF)


def combine_kernel(hot_ref, ids_ref, gate_ref, back_ref, hot_rows_ref, hot_more_ref, out_ref):
    ids, gates, hot = ids_ref[...], gate_ref[...], hot_ref[0]
    mask = slot_mask(ids, hot)
    column = lax.broadcasted_iota(I32, (TOK, EXPERTS), 1)
    per_expert = jnp.zeros((TOK, EXPERTS), I32)
    hot_gate = jnp.zeros((TOK, 1), I32)
    for k in range(4):
        ids_k, gates_k = ids[:, k : k + 1], gates[:, k : k + 1]
        per_expert = per_expert + jnp.where(ids_k == column, gates_k, 0)
        hot_gate = hot_gate + jnp.where(ids_k == hot, gates_k, 0)
    high = lax.shift_right_logical(per_expert, 8).astype(F32).astype(BF)
    low = jnp.bitwise_and(per_expert, 255).astype(F32).astype(BF)
    spread = expand()
    high = jnp.where(mask, dot(high, spread), 0.0).astype(BF)
    low = jnp.where(mask, dot(low, spread), 0.0).astype(BF)
    back = back_ref[...]
    mixed = dot(high, back) * (1.0 / 256.0) + dot(low, back) * (1.0 / 65536.0)
    hot_scale = hot_gate.astype(F32) * (1.0 / 65536.0)
    hot_rows = hot_rows_ref[...].astype(F32) + hot_more_ref[...].astype(F32)
    out_ref[...] = (mixed + hot_scale * hot_rows).astype(BF)


def silu_mul(gated, upward):
    return (gated / (1.0 + jnp.exp(-gated)) * upward).astype(BF)


def down_block(value):
    return jnp.concatenate([value[:, j * 128 : (j + 1) * 128] for j in range(value.shape[1] // 128)], 0)


def pack_kernel(owner_ref, gate_ref, up_ref, down_ref, out_ref, hot_ref):
    owner = owner_ref[0] == 1
    for q in range(4):
        rows = slice(q * 32, (q + 1) * 32)
        blocks = [down_ref[0, j * 128 + q * 32 : j * 128 + (q + 1) * 32, :] for j in range(6)]
        for i, part in enumerate((gate_ref[0, rows, :], up_ref[0, rows, :], jnp.concatenate(blocks, 1))):
            out_ref[q, i * 32 : (i + 1) * 32, :] = part
            hot_ref[q, i * 32 : (i + 1) * 32, :] = jnp.where(owner, part, jnp.zeros_like(part))


def own_kernel(place_ref, rows_ref, *refs):
    pieces, out_ref, (gate, up, down, sems, hidden) = refs[:18], refs[18], refs[19:]
    copies = ([], [], [])
    for i, piece in enumerate(pieces):
        spot, xs = (i, slice(0, 4)) if i < 14 else (14 + (i - 14) // 2, slice(i % 2 * 2, i % 2 * 2 + 2))
        zlo, zhi, core = (place_ref[spot * 3 + j] for j in range(3))
        for part, target in enumerate((gate, up, down)):
            view, spot_view = piece.at[:, pl.ds(part * 32, 32)], target.at[zlo, xs, core, zhi]
            copies[part].append(pltpu.make_async_copy(view, spot_view, sems.at[part * 18 + i]))
    for part in copies:
        for copy in part:
            copy.start()

    def arrive(part):
        for copy in copies[part]:
            copy.wait()

    arrive(0)
    for n in range(3):
        cols = slice(n * 256, (n + 1) * 256)
        gated = dot(rows_ref[...], gate[:, :, :, :, :, cols].reshape(WIDTH, 256))
        if n == 0:
            arrive(1)
        upward = dot(rows_ref[...], up[:, :, :, :, :, cols].reshape(WIDTH, 256))
        hidden[:, cols] = silu_mul(gated, upward)
    arrive(2)
    for d in range(0, 16, 2):
        pair = [down_block(down[d // 8, d // 2 % 4, c].reshape(128, FF)) for c in range(2)]
        out_ref[:, d * 128 : (d + 2) * 128] = dot(hidden[...], jnp.concatenate(pair, 1)).astype(BF)


def hot_kernel(mine_ref, theirs_ref, w_ref, out_ref, send_ref, tok, hidden):
    tok[0:TOK, :] = mine_ref[...]
    tok[TOK:, :] = theirs_ref[...]

    def part(d, first):
        zlo, x, core = d // 8, d // 2 % 4, d % 2
        return [w_ref[x, core, y, zlo, first : first + 32, :] for y in range(4)]

    gated = dot(tok[...], jnp.concatenate(sum([part(d, 0) for d in range(16)], []), 0))
    upward = dot(tok[...], jnp.concatenate(sum([part(d, 32) for d in range(16)], []), 0))
    hidden[...] = silu_mul(gated, upward)
    for d in range(0, 16, 2):
        pair = [down_block(jnp.concatenate(part(d + c, 64), 0)) for c in range(2)]
        rows = dot(hidden[...], jnp.concatenate(pair, 1)).astype(BF)
        out_ref[:, d * 128 : (d + 2) * 128] = rows[0:TOK]
        send_ref[:, d * 128 : (d + 2) * 128] = rows[TOK:]


def z_index(z):
    return (z % 2) * 4 + (z % 8) // 2


def z_shift(value, step):
    pairs = [(z_index(z), z_index(z + step)) for z in range(8)]
    return lax.ppermute(value, ("zlo", "zhi"), pairs)


def turn(value, axis, step):
    size = SIZES[AXES.index(axis)]
    return lax.ppermute(value, axis, [(i, (i + step) % size) for i in range(size)])


def other_core(value):
    return turn(value, "core", 1)


def after(value, *others):
    return lax.optimization_barrier((value, *others))[0]


def gather_ring(own, between):
    up = down = own
    found = []
    for step in range(4):
        waits = between(step, (up, down))
        up, down = after(up, *waits), after(down, *waits)
        if step == 3:
            up, down = up[:2], down[2:]
        up, down = z_shift(up, 1), z_shift(down, -1)
        found += [up, down]
    both = []
    for piece in [own] + found[:6]:
        both += [piece, other_core(piece)]
    return both + found[6:] + [other_core(piece) for piece in found[6:]]


def places():
    z = lax.axis_index("zhi") * 2 + lax.axis_index("zlo")
    core = lax.axis_index("core")
    out = []
    for step in (0, -1, 1, -2, 2, -3, 3, 4):
        from_z = lax.rem(z + step + 8, 8)
        for which in (core, 1 - core):
            out += [lax.rem(from_z, 2), from_z // 2, which]
    return jnp.stack(out).astype(I32)


def hot_near(masked, wait):
    mine = after(lax.psum_scatter(masked, "y", scatter_dimension=0, tiled=False), wait)
    return mine, turn(mine, "zhi", 1), turn(mine, "zhi", -1)


def hot_slices(parts, hot, waits):
    mine, below, above = parts
    across = turn(after(below, *waits), "zhi", 1)
    gap = lax.rem(hot % 4 - lax.axis_index("zhi") + 4, 4)
    mine = lax.select_n(gap, mine, above, across, below)
    zlo = lax.axis_index("zlo")
    low, high = mine[:, : FF // 2], mine[:, FF // 2 :]
    kept = jnp.where(zlo == 0, low, high)
    theirs = turn(jnp.where(zlo == 0, high, low), "zlo", 1)
    return jnp.stack([jnp.where(zlo == 0, kept, theirs), jnp.where(zlo == 0, theirs, kept)])


def on_device(tokens, expert_ids, gate_fixed, hot_ids, w_gate, w_up, w_down):
    owner = lax.axis_index("y") * 4 + lax.axis_index("zhi") == hot_ids[0]
    packed_shape = jax.ShapeDtypeStruct((4, 96, FF), BF)
    packed, masked = pl.pallas_call(
        pack_kernel,
        out_shape=(packed_shape, packed_shape),
        in_specs=[SMEM] + vmem(3),
        out_specs=(pl.BlockSpec(), pl.BlockSpec()),
        compiler_params=PARAMS,
    )(owner.astype(I32)[None], w_gate, w_up, w_down)
    spread = lax.all_to_all(packed, "zhi", split_axis=0, concat_axis=0, tiled=True)
    turned = lax.all_to_all(spread, "x", split_axis=0, concat_axis=0, tiled=True)
    near = hot_near(masked, spread)
    outgoing = pl.pallas_call(
        dispatch_kernel,
        out_shape=jax.ShapeDtypeStruct((SLOTS, WIDTH), BF),
        in_specs=[SMEM] + vmem(2),
        out_specs=pl.BlockSpec(),
        compiler_params=PARAMS,
    )(hot_ids, expert_ids, tokens)
    arrived = lax.all_to_all(outgoing, ("y", "x"), split_axis=0, concat_axis=0, tiled=True)
    slices = []

    def between(step, lanes):
        if step == 0:
            slices.append(hot_slices(near, hot_ids[0], (turned,)))
            return slices
        return (arrived,) if step == 3 else ()

    pieces = gather_ring(turned, between)
    hot_weights = lax.all_gather(slices[0], ("x", "core", "y"), axis=0, tiled=False).reshape(4, 2, 4, 2, 96, FF // 2)
    near_tokens = turn(after(tokens, *pieces[14:16]), "zlo", 1)
    result = pl.pallas_call(
        own_kernel,
        out_shape=jax.ShapeDtypeStruct((SLOTS, WIDTH), BF),
        in_specs=[SMEM] + vmem(1) + anywhere(18),
        out_specs=pl.BlockSpec(),
        scratch_shapes=[pltpu.VMEM((2, 4, 2, 4, 32, FF), BF)] * 3
        + [
            pltpu.SemaphoreType.DMA((54,)),
            pltpu.VMEM((SLOTS, FF), BF),
        ],
        compiler_params=PARAMS,
        cost_estimate=pl.CostEstimate(flops=4_900_000_000, bytes_accessed=14_000_000, transcendentals=400_000),
    )(places(), arrived, *pieces)
    returned = lax.all_to_all(result, ("y", "x"), split_axis=0, concat_axis=0, tiled=True)
    hot_rows, hot_send = pl.pallas_call(
        hot_kernel,
        out_shape=(jax.ShapeDtypeStruct((TOK, WIDTH), BF),) * 2,
        in_specs=vmem(3),
        out_specs=tuple(vmem(2)),
        scratch_shapes=[pltpu.VMEM((2 * TOK, WIDTH), BF), pltpu.VMEM((2 * TOK, FF // 2), BF)],
        compiler_params=PARAMS,
        cost_estimate=pl.CostEstimate(flops=1_300_000_000, bytes_accessed=7_000_000, transcendentals=100_000),
    )(tokens, near_tokens, hot_weights)
    return pl.pallas_call(
        combine_kernel,
        out_shape=jax.ShapeDtypeStruct((TOK, WIDTH), BF),
        in_specs=[SMEM] + vmem(5),
        out_specs=vmem(1)[0],
        compiler_params=PARAMS,
    )(hot_ids, expert_ids, gate_fixed, returned, hot_rows, turn(hot_send, "zlo", 1))


def solution(mesh):
    fine = Mesh(mesh.devices.reshape(SIZES), AXES)
    rows = P(("zlo", "x", "core", "y", "zhi"), None)
    slices = ("zlo", "x", "core")
    return jax.shard_map(
        on_device,
        mesh=fine,
        in_specs=(
            rows,
            rows,
            rows,
            P(),
            P(("y", "zhi"), slices, None),
            P(("y", "zhi"), slices, None),
            P(("y", "zhi"), None, slices),
        ),
        out_specs=rows,
        check_vma=False,
    )
```

```python
import jax
import jax.numpy as jnp
from jax import lax
from jax.experimental import pallas as pl
from jax.experimental.pallas import tpu as pltpu
from jax.sharding import Mesh, PartitionSpec as P

AXES = ("zlo", "x", "core", "y", "zhi")
SIZES = (2, 4, 2, 4, 4)
TOK, WIDTH, FF, EXPERTS, CAP = 128, 2048, 768, 16, 32
SLOTS = EXPERTS * CAP
BF, F32, I32 = jnp.bfloat16, jnp.float32, jnp.int32


def dot(a, b):
    return jnp.dot(a, b, preferred_element_type=F32)


def vmem(count):
    return [pl.BlockSpec(memory_space=pltpu.VMEM)] * count


def anywhere(count):
    return [pl.BlockSpec(memory_space=pltpu.HBM)] * count


SMEM = pl.BlockSpec(memory_space=pltpu.SMEM)
PARAMS = pltpu.CompilerParams(vmem_limit_bytes=24 * 2**20)


def expand():
    expert = lax.broadcasted_iota(I32, (EXPERTS, SLOTS), 0)
    slot = lax.broadcasted_iota(I32, (EXPERTS, SLOTS), 1)
    return (lax.shift_right_logical(slot, 5) == expert).astype(F32).astype(BF)


def slot_mask(ids, hot):
    column = lax.broadcasted_iota(I32, (TOK, EXPERTS), 1)
    member = ids[:, 0:1] == column
    for k in range(1, 4):
        member = jnp.logical_or(member, ids[:, k : k + 1] == column)
    row = lax.broadcasted_iota(I32, (TOK, TOK), 0)
    col = lax.broadcasted_iota(I32, (TOK, TOK), 1)
    earlier = (col < row).astype(F32).astype(BF)
    rank = dot(earlier, member.astype(F32).astype(BF))
    rank = jnp.where(jnp.logical_and(member, column != hot), rank, -1.0)
    wide = dot(rank.astype(BF), expand())
    place = jnp.bitwise_and(lax.broadcasted_iota(I32, (TOK, SLOTS), 1), CAP - 1)
    return wide == place.astype(F32)


def dispatch_kernel(hot_ref, ids_ref, tok_ref, out_ref):
    mask = slot_mask(ids_ref[...], hot_ref[0]).astype(F32).astype(BF)
    out_ref[...] = lax.dot_general(
        mask, tok_ref[...], (((0,), (0,)), ((), ())), preferred_element_type=F32
    ).astype(BF)


def combine_kernel(hot_ref, ids_ref, gate_ref, back_ref, hot_rows_ref, hot_more_ref, out_ref):
    ids, gates, hot = ids_ref[...], gate_ref[...], hot_ref[0]
    mask = slot_mask(ids, hot)
    column = lax.broadcasted_iota(I32, (TOK, EXPERTS), 1)
    per_expert = jnp.zeros((TOK, EXPERTS), I32)
    hot_gate = jnp.zeros((TOK, 1), I32)
    for k in range(4):
        ids_k, gates_k = ids[:, k : k + 1], gates[:, k : k + 1]
        per_expert = per_expert + jnp.where(ids_k == column, gates_k, 0)
        hot_gate = hot_gate + jnp.where(ids_k == hot, gates_k, 0)
    high = lax.shift_right_logical(per_expert, 8).astype(F32).astype(BF)
    low = jnp.bitwise_and(per_expert, 255).astype(F32).astype(BF)
    spread = expand()
    high = jnp.where(mask, dot(high, spread), 0.0).astype(BF)
    low = jnp.where(mask, dot(low, spread), 0.0).astype(BF)
    back = back_ref[...]
    mixed = dot(high, back) * (1.0 / 256.0) + dot(low, back) * (1.0 / 65536.0)
    hot_scale = hot_gate.astype(F32) * (1.0 / 65536.0)
    hot_rows = hot_rows_ref[...].astype(F32) + hot_more_ref[...].astype(F32)
    out_ref[...] = (mixed + hot_scale * hot_rows).astype(BF)


def silu_mul(gated, upward):
    return (gated / (1.0 + jnp.exp(-gated)) * upward).astype(BF)


def down_block(value):
    return jnp.concatenate([value[:, j * 128 : (j + 1) * 128] for j in range(value.shape[1] // 128)], 0)


def pack_kernel(owner_ref, gate_ref, up_ref, down_ref, out_ref, hot_ref):
    owner = owner_ref[0] == 1
    for q in range(4):
        rows = slice(q * 32, (q + 1) * 32)
        blocks = [down_ref[0, j * 128 + q * 32 : j * 128 + (q + 1) * 32, :] for j in range(6)]
        for i, part in enumerate((gate_ref[0, rows, :], up_ref[0, rows, :], jnp.concatenate(blocks, 1))):
            out_ref[q, i * 32 : (i + 1) * 32, :] = part
            hot_ref[q, i * 32 : (i + 1) * 32, :] = jnp.where(owner, part, jnp.zeros_like(part))


def own_kernel(place_ref, rows_ref, *refs):
    pieces, out_ref, (gate, up, down, sems, hidden) = refs[:18], refs[18], refs[19:]
    copies = ([], [], [])
    for i, piece in enumerate(pieces):
        spot, xs = (i, slice(0, 4)) if i < 14 else (14 + (i - 14) // 2, slice(i % 2 * 2, i % 2 * 2 + 2))
        zlo, zhi, core = (place_ref[spot * 3 + j] for j in range(3))
        for part, target in enumerate((gate, up, down)):
            view, spot_view = piece.at[:, pl.ds(part * 32, 32)], target.at[zlo, xs, core, zhi]
            copies[part].append(pltpu.make_async_copy(view, spot_view, sems.at[part * 18 + i]))
    for part in copies:
        for copy in part:
            copy.start()

    def arrive(part):
        for copy in copies[part]:
            copy.wait()

    arrive(0)
    for n in range(3):
        cols = slice(n * 256, (n + 1) * 256)
        gated = dot(rows_ref[...], gate[:, :, :, :, :, cols].reshape(WIDTH, 256))
        if n == 0:
            arrive(1)
        upward = dot(rows_ref[...], up[:, :, :, :, :, cols].reshape(WIDTH, 256))
        hidden[:, cols] = silu_mul(gated, upward)
    arrive(2)
    for d in range(0, 16, 2):
        pair = [down_block(down[d // 8, d // 2 % 4, c].reshape(128, FF)) for c in range(2)]
        out_ref[:, d * 128 : (d + 2) * 128] = dot(hidden[...], jnp.concatenate(pair, 1)).astype(BF)


def hot_kernel(mine_ref, theirs_ref, w_ref, out_ref, send_ref, tok, hidden):
    tok[0:TOK, :] = mine_ref[...]
    tok[TOK:, :] = theirs_ref[...]

    def part(d, first):
        zlo, x, core = d // 8, d // 2 % 4, d % 2
        return [w_ref[x, core, y, zlo, first : first + 32, :] for y in range(4)]

    gated = dot(tok[...], jnp.concatenate(sum([part(d, 0) for d in range(16)], []), 0))
    upward = dot(tok[...], jnp.concatenate(sum([part(d, 32) for d in range(16)], []), 0))
    hidden[...] = silu_mul(gated, upward)
    for d in range(0, 16, 2):
        pair = [down_block(jnp.concatenate(part(d + c, 64), 0)) for c in range(2)]
        rows = dot(hidden[...], jnp.concatenate(pair, 1)).astype(BF)
        out_ref[:, d * 128 : (d + 2) * 128] = rows[0:TOK]
        send_ref[:, d * 128 : (d + 2) * 128] = rows[TOK:]


def z_index(z):
    return (z % 2) * 4 + (z % 8) // 2


def z_shift(value, step):
    pairs = [(z_index(z), z_index(z + step)) for z in range(8)]
    return lax.ppermute(value, ("zlo", "zhi"), pairs)


def turn(value, axis, step):
    size = SIZES[AXES.index(axis)]
    return lax.ppermute(value, axis, [(i, (i + step) % size) for i in range(size)])


def other_core(value):
    return turn(value, "core", 1)


def after(value, *others):
    return lax.optimization_barrier((value, *others))[0]


def gather_ring(own, waits):
    up = down = own
    found = []
    for step in range(4):
        if step in waits:
            up, down = after(up, *waits[step]), after(down, *waits[step])
        if step == 3:
            up, down = up[:2], down[2:]
        up, down = z_shift(up, 1), z_shift(down, -1)
        found += [up, down]
    both = []
    for piece in [own] + found[:6]:
        both += [piece, other_core(piece)]
    return both + found[6:] + [other_core(piece) for piece in found[6:]]


def places():
    z = lax.axis_index("zhi") * 2 + lax.axis_index("zlo")
    core = lax.axis_index("core")
    out = []
    for step in (0, -1, 1, -2, 2, -3, 3, 4):
        from_z = lax.rem(z + step + 8, 8)
        for which in (core, 1 - core):
            out += [lax.rem(from_z, 2), from_z // 2, which]
    return jnp.stack(out).astype(I32)


def hot_slices(masked, hot, wait, waits):
    mine = after(lax.psum_scatter(masked, "y", scatter_dimension=0, tiled=False), wait)
    zlo = lax.axis_index("zlo")
    low, high = mine[:, : FF // 2], mine[:, FF // 2 :]
    kept = jnp.where(zlo == 0, low, high)
    theirs = turn(jnp.where(zlo == 0, high, low), "zlo", 1)
    both = jnp.stack([jnp.where(zlo == 0, kept, theirs), jnp.where(zlo == 0, theirs, kept)])
    below, above = turn(both, "zhi", 1), turn(both, "zhi", -1)
    across = turn(after(below, *waits), "zhi", 1)
    gap = lax.rem(lax.axis_index("zhi") - hot % 4 + 4, 4)
    return lax.select_n(gap, both, below, across, above)


def on_device(tokens, expert_ids, gate_fixed, hot_ids, w_gate, w_up, w_down):
    owner = lax.axis_index("y") * 4 + lax.axis_index("zhi") == hot_ids[0]
    packed_shape = jax.ShapeDtypeStruct((4, 96, FF), BF)
    packed, masked = pl.pallas_call(
        pack_kernel,
        out_shape=(packed_shape, packed_shape),
        in_specs=[SMEM] + vmem(3),
        out_specs=(pl.BlockSpec(), pl.BlockSpec()),
        compiler_params=PARAMS,
    )(owner.astype(I32)[None], w_gate, w_up, w_down)
    outgoing = pl.pallas_call(
        dispatch_kernel,
        out_shape=jax.ShapeDtypeStruct((SLOTS, WIDTH), BF),
        in_specs=[SMEM] + vmem(2),
        out_specs=pl.BlockSpec(),
        compiler_params=PARAMS,
    )(hot_ids, expert_ids, tokens)
    spread = lax.all_to_all(packed, "zhi", split_axis=0, concat_axis=0, tiled=True)
    turned = lax.all_to_all(spread, "x", split_axis=0, concat_axis=0, tiled=True)
    arrived = lax.all_to_all(outgoing, ("y", "x"), split_axis=0, concat_axis=0, tiled=True)
    slices = hot_slices(masked, hot_ids[0], spread, (turned, outgoing))
    pieces = gather_ring(turned, {0: (slices,), 3: (arrived,)})
    hot_weights = lax.all_gather(slices, ("x", "core", "y"), axis=0, tiled=False).reshape(4, 2, 4, 2, 96, FF // 2)
    near_tokens = turn(after(tokens, *pieces[14:16]), "zlo", 1)
    result = pl.pallas_call(
        own_kernel,
        out_shape=jax.ShapeDtypeStruct((SLOTS, WIDTH), BF),
        in_specs=[SMEM] + vmem(1) + anywhere(18),
        out_specs=pl.BlockSpec(),
        scratch_shapes=[pltpu.VMEM((2, 4, 2, 4, 32, FF), BF)] * 3
        + [
            pltpu.SemaphoreType.DMA((54,)),
            pltpu.VMEM((SLOTS, FF), BF),
        ],
        compiler_params=PARAMS,
        cost_estimate=pl.CostEstimate(flops=4_900_000_000, bytes_accessed=14_000_000, transcendentals=400_000),
    )(places(), arrived, *pieces)
    returned = lax.all_to_all(result, ("y", "x"), split_axis=0, concat_axis=0, tiled=True)
    hot_rows, hot_send = pl.pallas_call(
        hot_kernel,
        out_shape=(jax.ShapeDtypeStruct((TOK, WIDTH), BF),) * 2,
        in_specs=vmem(3),
        out_specs=tuple(vmem(2)),
        scratch_shapes=[pltpu.VMEM((2 * TOK, WIDTH), BF), pltpu.VMEM((2 * TOK, FF // 2), BF)],
        compiler_params=PARAMS,
        cost_estimate=pl.CostEstimate(flops=1_300_000_000, bytes_accessed=7_000_000, transcendentals=100_000),
    )(tokens, near_tokens, hot_weights)
    return pl.pallas_call(
        combine_kernel,
        out_shape=jax.ShapeDtypeStruct((TOK, WIDTH), BF),
        in_specs=[SMEM] + vmem(5),
        out_specs=vmem(1)[0],
        compiler_params=PARAMS,
    )(hot_ids, expert_ids, gate_fixed, returned, hot_rows, turn(hot_send, "zlo", 1))


def solution(mesh):
    fine = Mesh(mesh.devices.reshape(SIZES), AXES)
    rows = P(("zlo", "x", "core", "y", "zhi"), None)
    slices = ("zlo", "x", "core")
    return jax.shard_map(
        on_device,
        mesh=fine,
        in_specs=(
            rows,
            rows,
            rows,
            P(),
            P(("y", "zhi"), slices, None),
            P(("y", "zhi"), slices, None),
            P(("y", "zhi"), None, slices),
        ),
        out_specs=rows,
        check_vma=False,
    )
```

```python
import jax
import jax.numpy as jnp
from jax import lax
from jax.experimental import pallas as pl
from jax.experimental.pallas import tpu as pltpu
from jax.sharding import Mesh, PartitionSpec as P

AXES = ("zlo", "x", "core", "y", "zhi")
SIZES = (2, 4, 2, 4, 4)
TOK, WIDTH, FF, EXPERTS, CAP = 128, 2048, 768, 16, 32
SLOTS = EXPERTS * CAP
BF, F32, I32 = jnp.bfloat16, jnp.float32, jnp.int32


def dot(a, b):
    return jnp.dot(a, b, preferred_element_type=F32)


def vmem(count):
    return [pl.BlockSpec(memory_space=pltpu.VMEM)] * count


def anywhere(count):
    return [pl.BlockSpec(memory_space=pltpu.HBM)] * count


SMEM = pl.BlockSpec(memory_space=pltpu.SMEM)
PARAMS = pltpu.CompilerParams(vmem_limit_bytes=24 * 2**20)


def expand():
    expert = lax.broadcasted_iota(I32, (EXPERTS, SLOTS), 0)
    slot = lax.broadcasted_iota(I32, (EXPERTS, SLOTS), 1)
    return (lax.shift_right_logical(slot, 5) == expert).astype(F32).astype(BF)


def slot_mask(ids, hot):
    column = lax.broadcasted_iota(I32, (TOK, EXPERTS), 1)
    member = ids[:, 0:1] == column
    for k in range(1, 4):
        member = jnp.logical_or(member, ids[:, k : k + 1] == column)
    row = lax.broadcasted_iota(I32, (TOK, TOK), 0)
    col = lax.broadcasted_iota(I32, (TOK, TOK), 1)
    earlier = (col < row).astype(F32).astype(BF)
    rank = dot(earlier, member.astype(F32).astype(BF))
    rank = jnp.where(jnp.logical_and(member, column != hot), rank, -1.0)
    wide = dot(rank.astype(BF), expand())
    place = jnp.bitwise_and(lax.broadcasted_iota(I32, (TOK, SLOTS), 1), CAP - 1)
    return wide == place.astype(F32)


def dispatch_kernel(hot_ref, ids_ref, tok_ref, out_ref):
    mask = slot_mask(ids_ref[...], hot_ref[0]).astype(F32).astype(BF)
    out_ref[...] = lax.dot_general(
        mask, tok_ref[...], (((0,), (0,)), ((), ())), preferred_element_type=F32
    ).astype(BF)


def combine_kernel(hot_ref, ids_ref, gate_ref, back_ref, hot_rows_ref, hot_more_ref, out_ref):
    ids, gates, hot = ids_ref[...], gate_ref[...], hot_ref[0]
    mask = slot_mask(ids, hot)
    column = lax.broadcasted_iota(I32, (TOK, EXPERTS), 1)
    per_expert = jnp.zeros((TOK, EXPERTS), I32)
    hot_gate = jnp.zeros((TOK, 1), I32)
    for k in range(4):
        ids_k, gates_k = ids[:, k : k + 1], gates[:, k : k + 1]
        per_expert = per_expert + jnp.where(ids_k == column, gates_k, 0)
        hot_gate = hot_gate + jnp.where(ids_k == hot, gates_k, 0)
    high = lax.shift_right_logical(per_expert, 8).astype(F32).astype(BF)
    low = jnp.bitwise_and(per_expert, 255).astype(F32).astype(BF)
    spread = expand()
    high = jnp.where(mask, dot(high, spread), 0.0).astype(BF)
    low = jnp.where(mask, dot(low, spread), 0.0).astype(BF)
    back = back_ref[...]
    sums = dot(jnp.concatenate([high, low], 0), back)
    mixed = sums[:TOK] * (1.0 / 256.0) + sums[TOK:] * (1.0 / 65536.0)
    hot_scale = hot_gate.astype(F32) * (1.0 / 65536.0)
    hot_rows = hot_rows_ref[...].astype(F32) + hot_more_ref[...].astype(F32)
    out_ref[...] = (mixed + hot_scale * hot_rows).astype(BF)


def silu_mul(gated, upward):
    return (gated / (1.0 + jnp.exp(-gated)) * upward).astype(BF)


def down_block(value):
    return jnp.concatenate([value[:, j * 128 : (j + 1) * 128] for j in range(value.shape[1] // 128)], 0)


def pack_kernel(owner_ref, gate_ref, up_ref, down_ref, out_ref, hot_ref):
    owner = owner_ref[0] == 1
    for q in range(4):
        rows = slice(q * 32, (q + 1) * 32)
        blocks = [down_ref[0, j * 128 + q * 32 : j * 128 + (q + 1) * 32, :] for j in range(6)]
        for i, part in enumerate((gate_ref[0, rows, :], up_ref[0, rows, :], jnp.concatenate(blocks, 1))):
            out_ref[q, i * 32 : (i + 1) * 32, :] = part
            hot_ref[q, i * 32 : (i + 1) * 32, :] = jnp.where(owner, part, jnp.zeros_like(part))


def own_kernel(place_ref, rows_ref, *refs):
    pieces, out_ref, (gate, up, down, sems, hidden) = refs[:18], refs[18], refs[19:]
    copies = ([], [], [])
    for i, piece in enumerate(pieces):
        spot, xs = (i, slice(0, 4)) if i < 14 else (14 + (i - 14) // 2, slice(i % 2 * 2, i % 2 * 2 + 2))
        zlo, zhi, core = (place_ref[spot * 3 + j] for j in range(3))
        for part, target in enumerate((gate, up, down)):
            view, spot_view = piece.at[:, pl.ds(part * 32, 32)], target.at[zlo, xs, core, zhi]
            copies[part].append(pltpu.make_async_copy(view, spot_view, sems.at[part * 18 + i]))
    for part in copies:
        for copy in part:
            copy.start()

    def arrive(part):
        for copy in copies[part]:
            copy.wait()

    arrive(0)
    for n in range(3):
        cols = slice(n * 256, (n + 1) * 256)
        gated = dot(rows_ref[...], gate[:, :, :, :, :, cols].reshape(WIDTH, 256))
        if n == 0:
            arrive(1)
        upward = dot(rows_ref[...], up[:, :, :, :, :, cols].reshape(WIDTH, 256))
        hidden[:, cols] = silu_mul(gated, upward)
    arrive(2)
    for d in range(0, 16, 2):
        pair = [down_block(down[d // 8, d // 2 % 4, c].reshape(128, FF)) for c in range(2)]
        out_ref[:, d * 128 : (d + 2) * 128] = dot(hidden[...], jnp.concatenate(pair, 1)).astype(BF)


def hot_kernel(mine_ref, theirs_ref, w_ref, out_ref, send_ref, tok, hidden):
    tok[0:TOK, :] = mine_ref[...]
    tok[TOK:, :] = theirs_ref[...]

    def part(d, first):
        zlo, x, core = d // 8, d // 2 % 4, d % 2
        return [w_ref[x, core, y, zlo, first : first + 32, :] for y in range(4)]

    gated = dot(tok[...], jnp.concatenate(sum([part(d, 0) for d in range(16)], []), 0))
    upward = dot(tok[...], jnp.concatenate(sum([part(d, 32) for d in range(16)], []), 0))
    hidden[...] = silu_mul(gated, upward)
    for d in range(0, 16, 2):
        pair = [down_block(jnp.concatenate(part(d + c, 64), 0)) for c in range(2)]
        rows = dot(hidden[...], jnp.concatenate(pair, 1)).astype(BF)
        out_ref[:, d * 128 : (d + 2) * 128] = rows[0:TOK]
        send_ref[:, d * 128 : (d + 2) * 128] = rows[TOK:]


def z_index(z):
    return (z % 2) * 4 + (z % 8) // 2


def z_shift(value, step):
    pairs = [(z_index(z), z_index(z + step)) for z in range(8)]
    return lax.ppermute(value, ("zlo", "zhi"), pairs)


def turn(value, axis, step):
    size = SIZES[AXES.index(axis)]
    return lax.ppermute(value, axis, [(i, (i + step) % size) for i in range(size)])


def other_core(value):
    return turn(value, "core", 1)


def after(value, *others):
    return lax.optimization_barrier((value, *others))[0]


def gather_ring(own, waits):
    up = down = own
    found = []
    for step in range(4):
        if step in waits:
            up, down = after(up, *waits[step]), after(down, *waits[step])
        if step == 3:
            up, down = up[:2], down[2:]
        up, down = z_shift(up, 1), z_shift(down, -1)
        found += [up, down]
    both = []
    for piece in [own] + found[:6]:
        both += [piece, other_core(piece)]
    return both + found[6:] + [other_core(piece) for piece in found[6:]]


def places():
    z = lax.axis_index("zhi") * 2 + lax.axis_index("zlo")
    core = lax.axis_index("core")
    out = []
    for step in (0, -1, 1, -2, 2, -3, 3, 4):
        from_z = lax.rem(z + step + 8, 8)
        for which in (core, 1 - core):
            out += [lax.rem(from_z, 2), from_z // 2, which]
    return jnp.stack(out).astype(I32)


def hot_slices(masked, hot, wait, waits):
    mine = after(lax.psum_scatter(masked, "y", scatter_dimension=0, tiled=False), wait)
    zlo = lax.axis_index("zlo")
    low, high = mine[:, : FF // 2], mine[:, FF // 2 :]
    kept = jnp.where(zlo == 0, low, high)
    theirs = turn(jnp.where(zlo == 0, high, low), "zlo", 1)
    both = jnp.stack([jnp.where(zlo == 0, kept, theirs), jnp.where(zlo == 0, theirs, kept)])
    below, above = turn(both, "zhi", 1), turn(both, "zhi", -1)
    across = turn(after(below, *waits), "zhi", 1)
    gap = lax.rem(lax.axis_index("zhi") - hot % 4 + 4, 4)
    return lax.select_n(gap, both, below, across, above)


def on_device(tokens, expert_ids, gate_fixed, hot_ids, w_gate, w_up, w_down):
    owner = lax.axis_index("y") * 4 + lax.axis_index("zhi") == hot_ids[0]
    packed_shape = jax.ShapeDtypeStruct((4, 96, FF), BF)
    packed, masked = pl.pallas_call(
        pack_kernel,
        out_shape=(packed_shape, packed_shape),
        in_specs=[SMEM] + vmem(3),
        out_specs=(pl.BlockSpec(), pl.BlockSpec()),
        compiler_params=PARAMS,
    )(owner.astype(I32)[None], w_gate, w_up, w_down)
    outgoing = pl.pallas_call(
        dispatch_kernel,
        out_shape=jax.ShapeDtypeStruct((SLOTS, WIDTH), BF),
        in_specs=[SMEM] + vmem(2),
        out_specs=pl.BlockSpec(),
        compiler_params=PARAMS,
    )(hot_ids, expert_ids, tokens)
    spread = lax.all_to_all(packed, "zhi", split_axis=0, concat_axis=0, tiled=True)
    turned = lax.all_to_all(spread, "x", split_axis=0, concat_axis=0, tiled=True)
    arrived = lax.all_to_all(outgoing, ("y", "x"), split_axis=0, concat_axis=0, tiled=True)
    slices = hot_slices(masked, hot_ids[0], spread, (turned, outgoing))
    pieces = gather_ring(turned, {0: (slices,), 3: (arrived,)})
    hot_weights = lax.all_gather(slices, ("x", "core", "y"), axis=0, tiled=False).reshape(4, 2, 4, 2, 96, FF // 2)
    near_tokens = turn(after(tokens, *pieces[14:16]), "zlo", 1)
    result = pl.pallas_call(
        own_kernel,
        out_shape=jax.ShapeDtypeStruct((SLOTS, WIDTH), BF),
        in_specs=[SMEM] + vmem(1) + anywhere(18),
        out_specs=pl.BlockSpec(),
        scratch_shapes=[pltpu.VMEM((2, 4, 2, 4, 32, FF), BF)] * 3
        + [
            pltpu.SemaphoreType.DMA((54,)),
            pltpu.VMEM((SLOTS, FF), BF),
        ],
        compiler_params=PARAMS,
        cost_estimate=pl.CostEstimate(flops=4_900_000_000, bytes_accessed=14_000_000, transcendentals=400_000),
    )(places(), arrived, *pieces)
    returned = lax.all_to_all(result, ("y", "x"), split_axis=0, concat_axis=0, tiled=True)
    hot_rows, hot_send = pl.pallas_call(
        hot_kernel,
        out_shape=(jax.ShapeDtypeStruct((TOK, WIDTH), BF),) * 2,
        in_specs=vmem(3),
        out_specs=tuple(vmem(2)),
        scratch_shapes=[pltpu.VMEM((2 * TOK, WIDTH), BF), pltpu.VMEM((2 * TOK, FF // 2), BF)],
        compiler_params=PARAMS,
        cost_estimate=pl.CostEstimate(flops=1_300_000_000, bytes_accessed=7_000_000, transcendentals=100_000),
    )(tokens, near_tokens, hot_weights)
    return pl.pallas_call(
        combine_kernel,
        out_shape=jax.ShapeDtypeStruct((TOK, WIDTH), BF),
        in_specs=[SMEM] + vmem(5),
        out_specs=vmem(1)[0],
        compiler_params=PARAMS,
    )(hot_ids, expert_ids, gate_fixed, returned, hot_rows, turn(hot_send, "zlo", 1))


def solution(mesh):
    fine = Mesh(mesh.devices.reshape(SIZES), AXES)
    rows = P(("zlo", "x", "core", "y", "zhi"), None)
    slices = ("zlo", "x", "core")
    return jax.shard_map(
        on_device,
        mesh=fine,
        in_specs=(
            rows,
            rows,
            rows,
            P(),
            P(("y", "zhi"), slices, None),
            P(("y", "zhi"), slices, None),
            P(("y", "zhi"), None, slices),
        ),
        out_specs=rows,
        check_vma=False,
    )
```
